32 devices in a mesh: parts: 2 (over y), off: 4 (over z), depth: 2 (over x), shot: 2 (over core).
Axes of the slice: x: 2, y: 2, z: 4, core: 2. Of those that a mesh axis runs over, the one named last changes fastest.
Arguments:
- image: bfloat16 [64, 32, 32, 256], P('off', None, 'depth'), may hold values from -4 to 4
- offset_of: int32 [64], P('off'), may hold values from 0 to 63, each once
- background: bfloat16 [4, 32, 32, 256], P(('parts', 'shot'), 'off', 'depth'), parts along dimension 0, may hold values from -6 to 6
- wave_now: float32 [4, 32, 32, 256], P(('parts', 'shot'), 'off', 'depth'), parts along dimension 0, may hold values from -6 to 6
- wave_prev: float32 [4, 32, 32, 256], P(('parts', 'shot'), 'off', 'depth'), parts along dimension 0, may hold values from -6 to 6
- courant: float32 [32, 32, 256], P('off', 'depth'), may hold values from 0.02 to 0.15
Outputs:
- wave_next: float32 [4, 32, 32, 256], P(('parts', 'shot'), 'off', 'depth'), parts along dimension 0
The draws below stay inside these ranges and needn't reach their ends.
There are 2 independent parts, one for each index of `parts`. The reference program is written for one: setup_inputs(seed, part) draws one part's arguments, and reference() takes and returns one part's arrays. A program takes and returns all parts, laid end to end along the dimension named above; an argument that names none is the same for every part. Nothing has to cross between parts.
Inputs may be any that keep to these rules, and one draw needn't show every extreme that they name: Each value appears once; image column k holds offset offset_of[k] - 32 cells along x.
All inputs are finite; a program needn't handle non-finite values.
Results may differ from the reference program's by a relative error of at most 0.0003.
Values may be sent and summed in bfloat16 or wider, within the bound.
No kernel may reach another device: no remote copies, remote signals or barrier semaphores. Data moves between devices by JAX's collectives and lax.ppermute only.
A program may use at most 64 MiB of HBM per device.

```python
import math
import jax
import jax.numpy as jnp
from jax import lax

H = 64
NX = 256
NY = 32
NZ = 32
SHOTS = 2


def spiked(result, own_key, source, target, parts, factor):
    owner, partner = [(jnp.arange(result.shape[dim]) // (result.shape[dim] // parts)).reshape([-1 if axis == dim else 1 for axis in range(result.ndim)]) for dim in (source, target)]
    chosen = jax.random.permutation(own_key, parts)[partner]
    strong = (owner == chosen) | (owner == (partner + parts // 2) % parts)
    return jnp.where(strong, factor * result, result)


def block_levels(stream_key, shape, pieces, least, largest):
    def one(dim, parts):
        steps = jax.random.uniform(jax.random.fold_in(jax.random.fold_in(stream_key, 6), dim), (parts,), jnp.float32, least / len(pieces), largest / len(pieces))
        return jnp.repeat(jnp.exp(steps), shape[dim] // parts).reshape((-1,) + (1,) * (len(shape) - dim - 1))

    factor_of = one(*pieces[0])
    for cut in pieces[1:]:
        factor_of = factor_of * one(*cut)
    return factor_of


def normal_values(stream_key, extent, deviation, limit, cuts=(), dtype=jnp.bfloat16):
    level = block_levels(stream_key, extent, cuts, -0.22, 0.18) if cuts else 1.0
    entries = jax.random.normal(stream_key, extent, jnp.float32) * deviation * level
    return jnp.minimum(jnp.maximum(entries, -limit), limit).astype(dtype)


def heavy_noise(stream_key, shape, spread, reach, cuts, heavy, kind=jnp.bfloat16):
    values = spread * jax.random.normal(stream_key, shape, jnp.float32)
    if cuts:
        values = values * block_levels(stream_key, shape, cuts, -0.22, 0.18)
    return jnp.clip(spiked(values, jax.random.fold_in(stream_key, 3), *heavy), -reach, reach).astype(kind)


def setup_inputs(seed: int = 0, part: int = 0) -> dict:
    keys = jax.random.split(jax.random.key(seed), 7)
    part_keys = jax.random.split(jax.random.fold_in(keys[6], part), 7)
    return {
        "image": heavy_noise(keys[0], (H, NY, NZ, NX), 0.5, 4.0, ((0, 4), (2, 2)), (0, 1, 4, 2.0)),
        "offset_of": jax.random.permutation(keys[1], H).astype(jnp.int32),
        "background": normal_values(part_keys[2], (SHOTS, NY, NZ, NX), 1.0, 6.0, ((0, 2), (1, 4), (2, 2))),
        "wave_now": normal_values(part_keys[3], (SHOTS, NY, NZ, NX), 1.0, 6.0, ((0, 2), (1, 4), (2, 2)), jnp.float32),
        "wave_prev": normal_values(part_keys[4], (SHOTS, NY, NZ, NX), 1.0, 6.0, ((0, 2), (1, 4), (2, 2)), jnp.float32),
        "courant": jnp.clip(jnp.exp(math.log(0.15) - 2.014903 * jax.random.uniform(keys[5], (NY, NZ, NX), jnp.float32) ** block_levels(keys[5], (NY, NZ, NX), ((0, 4), (1, 2)), -0.2, 0.2)), 0.02, 0.15),
    }


STENCIL = (-205.0 / 72.0, 8.0 / 5.0, -1.0 / 5.0, 8.0 / 315.0, -1.0 / 560.0)


def laplace(padded, rows_y, rows_z, cols_x):
    extended = jnp.pad(padded, ((0, 0), (0, 0), (4, 4)))
    centre = extended[4:4 + rows_y, 4:4 + rows_z, 4:4 + cols_x]
    running = 3.0 * STENCIL[0] * centre
    for radius in range(1, 5):
        beside_all = extended[4 + radius:4 + radius + rows_y, 4:4 + rows_z, 4:4 + cols_x]
        beside_all = beside_all + extended[4 - radius:4 - radius + rows_y, 4:4 + rows_z, 4:4 + cols_x]
        beside_all = beside_all + extended[4:4 + rows_y, 4 + radius:4 + radius + rows_z, 4:4 + cols_x]
        beside_all = beside_all + extended[4:4 + rows_y, 4 - radius:4 - radius + rows_z, 4:4 + cols_x]
        beside_all = beside_all + extended[4:4 + rows_y, 4:4 + rows_z, 4 + radius:4 + radius + cols_x]
        beside_all = beside_all + extended[4:4 + rows_y, 4:4 + rows_z, 4 - radius:4 - radius + cols_x]
        running = running + STENCIL[radius] * beside_all
    return running


def reference(image, offset_of, background, wave_now, wave_prev, courant):
    half_span = H // 2

    def one_shot(inputs):
        backdrop, current, previous = inputs
        extended_bg = jnp.pad(backdrop, ((0, 0), (0, 0), (half_span, half_span)))

        def add_column(column, running):
            offset_cells = (offset_of[column] - half_span).astype(jnp.int32)
            image_col = lax.dynamic_index_in_dim(image, column, 0, keepdims=False)
            starts = (jnp.zeros((), jnp.int32), jnp.zeros((), jnp.int32), (half_span - offset_cells).astype(jnp.int32))
            shifted = lax.dynamic_slice(extended_bg, starts, (NY, NZ, NX))
            return running + image_col.astype(jnp.float32) * shifted.astype(jnp.float32)

        source = lax.fori_loop(0, H, add_column, jnp.zeros((NY, NZ, NX), jnp.float32))
        padded = jnp.pad(current, ((4, 4), (4, 4), (0, 0)))
        bending = laplace(padded, NY, NZ, NX)
        return 2.0 * current - previous + courant * (bending + source)

    return lax.map(one_shot, (background, wave_now, wave_prev))
```

```python
import functools

import jax
import jax.numpy as jnp
from jax import lax
from jax.experimental import pallas as pl
from jax.experimental.pallas import tpu as pltpu
from jax.sharding import PartitionSpec as P

STENCIL = (-205.0 / 72.0, 8.0 / 5.0, -1.0 / 5.0, 8.0 / 315.0, -1.0 / 560.0)
WIDTH = len(STENCIL) - 1

VMEM = pl.BlockSpec(memory_space=pltpu.VMEM)
SMEM = pl.BlockSpec(memory_space=pltpu.SMEM)
PARAMS = pltpu.CompilerParams(vmem_limit_bytes=32 * 2**20)


def source_kernel(half_span, slab_ref, offset_ref, image_ref, background_ref, out_ref):
    columns = image_ref.shape[0]
    rows, depth, width = background_ref.shape
    first_row = slab_ref[0] * rows
    lane = lax.broadcasted_iota(jnp.int32, (depth, width), 1)

    def add_column(column, running):
        cells = offset_ref[column] - half_span
        inside = (lane >= cells) & (lane < width + cells)
        amount = lax.rem(cells + width, width)
        result = []
        for row in range(rows):
            shifted = pltpu.roll(background_ref[row].astype(jnp.float32), amount, 1)
            shifted = jnp.where(inside, shifted, 0.0)
            result.append(
                running[row] + image_ref[column, first_row + row].astype(jnp.float32) * shifted
            )
        return tuple(result)

    zero = jnp.zeros((depth, width), jnp.float32)
    totals = lax.fori_loop(0, columns, add_column, (zero,) * rows, unroll=True)
    for row in range(rows):
        out_ref[row] = totals[row]


def source_of(image, offset_of, background, slab, half_span):
    return pl.pallas_call(
        functools.partial(source_kernel, half_span),
        out_shape=jax.ShapeDtypeStruct(background.shape, jnp.float32),
        in_specs=[SMEM, SMEM, VMEM, VMEM],
        out_specs=VMEM,
        compiler_params=PARAMS,
        cost_estimate=pl.CostEstimate(
            flops=2 * image.shape[0] * background.size,
            bytes_accessed=2 * image.shape[0] * background.size,
            transcendentals=0,
        ),
    )(slab.reshape(1), offset_of, image, background)


def step_kernel(
    ends_ref, now_ref, before_ref, after_ref, above_ref, below_ref, prev_ref, courant_ref, own_ref, out_ref, deep_ref
):
    rows, depth, width = now_ref.shape
    deep_ref[:, 2 * WIDTH : 2 * WIDTH + depth] = now_ref[...]
    deep_ref[:, WIDTH : 2 * WIDTH] = jnp.where(ends_ref[0] != 0, above_ref[...], 0.0)
    deep_ref[:, 2 * WIDTH + depth : 3 * WIDTH + depth] = jnp.where(
        ends_ref[1] != 0, below_ref[...], 0.0
    )
    lane = lax.broadcasted_iota(jnp.int32, (depth, width), 1)

    def layer(row):
        if row < 0:
            return before_ref[row + WIDTH]
        if row >= rows:
            return after_ref[row - rows]
        return now_ref[row]

    for row in range(rows):
        centre = now_ref[row]
        bending = 3.0 * STENCIL[0] * centre
        for radius in range(1, WIDTH + 1):
            beside = layer(row - radius) + layer(row + radius)
            beside = beside + deep_ref[row, 2 * WIDTH - radius : 2 * WIDTH - radius + depth]
            beside = beside + deep_ref[row, 2 * WIDTH + radius : 2 * WIDTH + radius + depth]
            left = jnp.where(lane >= radius, pltpu.roll(centre, radius, 1), 0.0)
            right = jnp.where(lane < width - radius, pltpu.roll(centre, width - radius, 1), 0.0)
            bending = bending + STENCIL[radius] * (beside + (left + right))
        out_ref[row] = 2.0 * centre - prev_ref[row] + courant_ref[row] * (bending + own_ref[row])


def neighbour_layers(cells, axis, dim):
    count = lax.axis_size(axis)
    here = lax.axis_index(axis)
    head = lax.slice_in_dim(cells, 0, WIDTH, axis=dim)
    tail = lax.slice_in_dim(cells, cells.shape[dim] - WIDTH, cells.shape[dim], axis=dim)
    if count == 2:
        other = lax.ppermute(jnp.where(here == 0, tail, head), axis, [(0, 1), (1, 0)])
        return other, other
    return (
        lax.ppermute(tail, axis, [(i, i + 1) for i in range(count - 1)]),
        lax.ppermute(head, axis, [(i + 1, i) for i in range(count - 1)]),
    )


def on_device(half_span, image, offset_of, background, wave_now, wave_prev, courant):
    groups = lax.axis_size("off")
    here = lax.axis_index("off").astype(jnp.int32)
    depth_at = lax.axis_index("depth")
    own_slab, now, prev = background[0], wave_now[0], wave_prev[0]

    slabs = [
        lax.ppermute(own_slab, "off", [(i, (i + step) % groups) for i in range(groups)])
        for step in range(1, groups)
    ]
    before, after = neighbour_layers(now, "off", 0)
    above, below = neighbour_layers(now, "depth", 1)
    ends = jnp.stack([depth_at != 0, depth_at != lax.axis_size("depth") - 1]).astype(jnp.int32)

    own = source_of(image, offset_of, own_slab, here, half_span)
    rows, depth, width = now.shape
    base = pl.pallas_call(
        step_kernel,
        out_shape=jax.ShapeDtypeStruct(now.shape, jnp.float32),
        in_specs=[SMEM] + [VMEM] * 8,
        out_specs=VMEM,
        scratch_shapes=[pltpu.VMEM((rows, depth + 4 * WIDTH, width), jnp.float32)],
        compiler_params=PARAMS,
        cost_estimate=pl.CostEstimate(
            flops=40 * now.size, bytes_accessed=24 * now.size, transcendentals=0
        ),
    )(ends, now, before, after, above, below, prev, courant, own)

    returned = []
    for step in range(1, groups):
        slab = lax.rem(here - step + groups, groups)
        part = source_of(image, offset_of, slabs[step - 1], slab, half_span)
        returned.append(
            lax.ppermute(part, "off", [(i, (i - step) % groups) for i in range(groups)])
        )
    stepped = base + courant * functools.reduce(jnp.add, returned)
    return stepped[None]


def solution(mesh):
    def whole(image, offset_of, background, wave_now, wave_prev, courant):
        return jax.shard_map(
            functools.partial(on_device, offset_of.shape[0] // 2),
            mesh=mesh,
            in_specs=(
                P("off", None, "depth", None),
                P("off"),
                P(("parts", "shot"), "off", "depth", None),
                P(("parts", "shot"), "off", "depth", None),
                P(("parts", "shot"), "off", "depth", None),
                P("off", "depth", None),
            ),
            out_specs=P(("parts", "shot"), "off", "depth", None),
            check_vma=False,
        )(image, offset_of, background, wave_now, wave_prev, courant)

    return whole
```

```python
import functools

import jax
import jax.numpy as jnp
from jax import lax
from jax.experimental import pallas as pl
from jax.experimental.pallas import tpu as pltpu
from jax.sharding import PartitionSpec as P

STENCIL = (-205.0 / 72.0, 8.0 / 5.0, -1.0 / 5.0, 8.0 / 315.0, -1.0 / 560.0)
WIDTH = len(STENCIL) - 1
LANES = 128
MIB = 2**20

VMEM = pl.BlockSpec(memory_space=pltpu.VMEM)
SMEM = pl.BlockSpec(memory_space=pltpu.SMEM)
ANY = pl.BlockSpec(memory_space=pl.ANY)
COST = pl.CostEstimate(flops=1000, bytes_accessed=1000, transcendentals=0)


def add_column(half_span, offset_ref, image_ref, background_ref, first_row, column, running):
    rows, depth, width = background_ref.shape
    cells = offset_ref[column] - half_span
    back = cells < 0
    turn = jnp.where(back, cells + LANES, cells)
    wrapped = lax.broadcasted_iota(jnp.int32, (depth, LANES), 1) < turn
    result = []
    for row in range(rows):
        turned = [
            pltpu.roll(background_ref[row, :, start : start + LANES], turn, 1)
            for start in range(0, width, LANES)
        ]
        zero = jnp.zeros_like(turned[0])
        ahead = [zero] + turned
        behind = turned + [zero]
        chosen = [jnp.where(back, b, a) for a, b in zip(ahead, behind)]
        shifted = [jnp.where(wrapped, a, b) for a, b in zip(chosen[:-1], chosen[1:])]
        factor = image_ref[column, first_row + row].astype(jnp.float32)
        result.append(running[row] + factor * jnp.concatenate(shifted, 1).astype(jnp.float32))
    return tuple(result)


def first_kernel(half_span, offset_ref, image_ref, background_ref, now_ref, out_ref, held_ref, layers_ref, cells_ref, slab_ref, arrived, sem):
    columns = image_ref.shape[0]
    rows, depth, width = slab_ref.shape
    before = (
        pltpu.make_async_copy(offset_ref, cells_ref, sem.at[0]),
        pltpu.make_async_copy(background_ref, slab_ref, sem.at[1]),
    )
    wave = pltpu.make_async_copy(now_ref, layers_ref, sem.at[2])
    copies = [
        pltpu.make_async_copy(image_ref.at[column], held_ref.at[column], arrived.at[column])
        for column in range(columns)
    ]
    for copy in before + (wave,) + tuple(copies):
        copy.start()
    for copy in before:
        copy.wait()
    first_row = lax.axis_index("off") * rows
    add = functools.partial(add_column, half_span, cells_ref, held_ref, slab_ref, first_row)
    totals = (jnp.zeros((depth, width), jnp.float32),) * rows
    for column, copy in enumerate(copies):
        copy.wait()
        totals = add(column, totals)
    for row in range(rows):
        out_ref[row] = totals[row]
    wave.wait()


def first_source(image, offset_of, background, now, half_span):
    return pl.pallas_call(
        functools.partial(first_kernel, half_span),
        out_shape=(
            pltpu.VMEM(background.shape, jnp.float32),
            pltpu.VMEM(image.shape, image.dtype),
            pltpu.VMEM(now.shape, now.dtype),
            pltpu.SMEM(offset_of.shape, offset_of.dtype),
        ),
        in_specs=[ANY] * 4,
        out_specs=(VMEM, VMEM, VMEM, SMEM),
        scratch_shapes=[
            pltpu.VMEM(background.shape, background.dtype),
            pltpu.SemaphoreType.DMA((image.shape[0],)),
            pltpu.SemaphoreType.DMA((3,)),
        ],
        compiler_params=pltpu.CompilerParams(vmem_limit_bytes=32 * MIB),
        cost_estimate=COST,
    )(*[pltpu.with_memory_space_constraint(x, pltpu.HBM) for x in (offset_of, image, background, now)])


def source_kernel(half_span, step, groups, offset_ref, image_ref, background_ref, now_ref, earlier_ref, out_ref):
    del earlier_ref
    rows, depth, width = background_ref.shape
    here = lax.axis_index("off")
    slab = lax.rem(here - step + groups, groups)
    add = functools.partial(
        add_column, half_span, offset_ref, image_ref, background_ref, slab * rows
    )
    totals = (jnp.zeros((depth, width), jnp.float32),) * rows
    for column in range(image_ref.shape[0]):
        totals = add(column, totals)
    for row in range(rows):
        out_ref[row] = totals[row]
    at = rows
    if step == 1:
        for layer in range(WIDTH):
            out_ref[at + layer] = jnp.where(here != 0, now_ref[layer], 0.0)
        at += WIDTH
    if step == groups - 1:
        for layer in range(WIDTH):
            out_ref[at + layer] = jnp.where(
                here != groups - 1, now_ref[rows - WIDTH + layer], 0.0
            )


def source_of(image, offset_of, background, now, earlier, step, groups, half_span):
    rows, depth, width = background.shape
    extra = WIDTH * ((step == 1) + (step == groups - 1))
    return pl.pallas_call(
        functools.partial(source_kernel, half_span, step, groups),
        out_shape=pltpu.VMEM((rows + extra, depth, width), jnp.float32),
        in_specs=[SMEM, VMEM, VMEM, VMEM, ANY],
        out_specs=VMEM,
        compiler_params=pltpu.CompilerParams(vmem_limit_bytes=32 * MIB),
        cost_estimate=COST,
    )(offset_of, image, background, now, earlier)


def step_kernel(now_ref, above_ref, below_ref, prev_ref, courant_ref, own_ref, out_ref, deep_ref):
    rows, depth, width = now_ref.shape
    at = lax.axis_index("depth")
    deep_ref[:, 2 * WIDTH : 2 * WIDTH + depth] = now_ref[...]
    deep_ref[:, WIDTH : 2 * WIDTH] = jnp.where(
        at != 0, above_ref[:, depth - WIDTH :], 0.0
    )
    deep_ref[:, 2 * WIDTH + depth : 3 * WIDTH + depth] = jnp.where(
        at != lax.axis_size("depth") - 1, below_ref[:, :WIDTH], 0.0
    )
    lane = lax.broadcasted_iota(jnp.int32, (depth, width), 1)
    for row in range(rows):
        centre = now_ref[row]
        bending = 3.0 * STENCIL[0] * centre
        for radius in range(1, WIDTH + 1):
            beside = deep_ref[row, 2 * WIDTH - radius : 2 * WIDTH - radius + depth]
            beside = beside + deep_ref[row, 2 * WIDTH + radius : 2 * WIDTH + radius + depth]
            if row >= radius:
                beside = beside + now_ref[row - radius]
            if row + radius < rows:
                beside = beside + now_ref[row + radius]
            left = jnp.where(lane >= radius, pltpu.roll(centre, radius, 1), 0.0)
            right = jnp.where(lane < width - radius, pltpu.roll(centre, width - radius, 1), 0.0)
            bending = bending + STENCIL[radius] * (beside + (left + right))
        out_ref[row] = 2.0 * centre - prev_ref[row] + courant_ref[row] * (bending + own_ref[row])


def deep_neighbours(cells):
    count = lax.axis_size("depth")
    if count == 2:
        other = lax.ppermute(cells, "depth", [(0, 1), (1, 0)])
        return other, other
    return (
        lax.ppermute(cells, "depth", [(i, i + 1) for i in range(count - 1)]),
        lax.ppermute(cells, "depth", [(i + 1, i) for i in range(count - 1)]),
    )


def on_device(half_span, image, offset_of, background, wave_now, wave_prev, courant):
    groups = lax.axis_size("off")
    own_slab, prev = background[0], wave_prev[0]

    slabs = {}
    for step in range(1, groups):
        slabs[step] = lax.ppermute(
            own_slab, "off", [(i, (i + step) % groups) for i in range(groups)]
        )
    above, below = deep_neighbours(wave_now[0])
    own, held, now, cells = first_source(image, offset_of, own_slab, wave_now[0], half_span)
    rows, depth, width = now.shape

    returned = []
    part = own
    for step in range(1, groups):
        part = source_of(held, cells, slabs[step], now, part, step, groups, half_span)
        back = [(i, (i - step) % groups) for i in range(groups)]
        returned.append(
            lax.ppermute(part.astype(jnp.float16), "off", back).astype(jnp.float32)
        )

    base = pl.pallas_call(
        step_kernel,
        out_shape=jax.ShapeDtypeStruct(now.shape, jnp.float32),
        in_specs=[VMEM] * 6,
        out_specs=VMEM,
        scratch_shapes=[pltpu.VMEM((rows, depth + 4 * WIDTH, width), jnp.float32)],
        compiler_params=pltpu.CompilerParams(vmem_limit_bytes=32 * MIB),
        cost_estimate=COST,
    )(now, above, below, prev, courant, own)

    after, before = returned[0][rows : rows + WIDTH], returned[-1][-WIDTH:]
    beside = jnp.concatenate([before, jnp.zeros_like(now), after], axis=0)
    sums = functools.reduce(jnp.add, [part[:rows] for part in returned])
    for radius in range(1, WIDTH + 1):
        sums = sums + STENCIL[radius] * (
            beside[WIDTH - radius : WIDTH - radius + rows]
            + beside[WIDTH + radius : WIDTH + radius + rows]
        )
    return (base + courant * sums)[None]


def solution(mesh):
    def whole(image, offset_of, background, wave_now, wave_prev, courant):
        half_span = offset_of.shape[0] // 2
        assert half_span < LANES and background.shape[-1] % LANES == 0
        return jax.shard_map(
            functools.partial(on_device, half_span),
            mesh=mesh,
            in_specs=(
                P("off", None, "depth", None),
                P("off"),
                P(("parts", "shot"), "off", "depth", None),
                P(("parts", "shot"), "off", "depth", None),
                P(("parts", "shot"), "off", "depth", None),
                P("off", "depth", None),
            ),
            out_specs=P(("parts", "shot"), "off", "depth", None),
            check_vma=False,
        )(image, offset_of, background, wave_now, wave_prev, courant)

    return whole
```

```python
import functools

import jax
import jax.numpy as jnp
from jax import lax
from jax.experimental import pallas as pl
from jax.experimental.pallas import tpu as pltpu
from jax.sharding import PartitionSpec as P

STENCIL = (-205.0 / 72.0, 8.0 / 5.0, -1.0 / 5.0, 8.0 / 315.0, -1.0 / 560.0)
WIDTH = len(STENCIL) - 1
LANES = 128
MIB = 2**20

VMEM = pl.BlockSpec(memory_space=pltpu.VMEM)
SMEM = pl.BlockSpec(memory_space=pltpu.SMEM)
ANY = pl.BlockSpec(memory_space=pl.ANY)
COST = pl.CostEstimate(flops=1000, bytes_accessed=1000, transcendentals=0)


def add_column(half_span, offset_ref, image_ref, background_ref, first_row, column, running):
    rows, depth, width = background_ref.shape
    cells = offset_ref[column] - half_span
    back = cells < 0
    turn = jnp.where(back, cells + LANES, cells)
    wrapped = lax.broadcasted_iota(jnp.int32, (depth, LANES), 1) < turn
    result = []
    for row in range(rows):
        turned = [
            pltpu.roll(background_ref[row, :, start : start + LANES], turn, 1)
            for start in range(0, width, LANES)
        ]
        zero = jnp.zeros_like(turned[0])
        ahead = [zero] + turned
        behind = turned + [zero]
        chosen = [jnp.where(back, b, a) for a, b in zip(ahead, behind)]
        shifted = [jnp.where(wrapped, a, b) for a, b in zip(chosen[:-1], chosen[1:])]
        factor = image_ref[column, first_row + row].astype(jnp.float32)
        result.append(running[row] + factor * jnp.concatenate(shifted, 1).astype(jnp.float32))
    return tuple(result)


def slab_sums(half_span, offset_ref, image_ref, background_ref, slab):
    rows, depth, width = background_ref.shape
    add = functools.partial(
        add_column, half_span, offset_ref, image_ref, background_ref, slab * rows
    )
    totals = (jnp.zeros((depth, width), jnp.float32),) * rows
    for column in range(image_ref.shape[0]):
        totals = add(column, totals)
    return totals


def move_kernel(*refs):
    count = (len(refs) - 1) // 2
    arrived = refs[-1]
    copies = [
        pltpu.make_async_copy(refs[i], refs[count + i], arrived.at[i]) for i in range(count)
    ]
    for copy in copies:
        copy.start()
    for copy in copies:
        copy.wait()


def moved(*pairs):
    return pl.pallas_call(
        move_kernel,
        out_shape=[space(x.shape, x.dtype) for x, space in pairs],
        in_specs=[ANY] * len(pairs),
        out_specs=[pl.BlockSpec(memory_space=space) for _, space in pairs],
        scratch_shapes=[pltpu.SemaphoreType.DMA((len(pairs),))],
        compiler_params=pltpu.CompilerParams(vmem_limit_bytes=32 * MIB),
        cost_estimate=COST,
    )(*[pltpu.with_memory_space_constraint(x, pltpu.HBM) for x, _ in pairs])


def source_kernel(half_span, step, groups, offset_ref, image_ref, background_ref, now_ref, earlier_ref, out_ref, *edge_refs):
    del earlier_ref
    rows, depth, width = background_ref.shape
    here = lax.axis_index("off")
    slab = lax.rem(here - step + groups, groups)
    totals = slab_sums(half_span, offset_ref, image_ref, background_ref, slab)
    for row in range(rows):
        out_ref[row] = totals[row]
    at = rows
    if step == 1:
        for layer in range(WIDTH):
            out_ref[at + layer] = jnp.where(here != 0, now_ref[layer], 0.0)
        at += WIDTH
    if step == groups - 1:
        for layer in range(WIDTH):
            out_ref[at + layer] = jnp.where(
                here != groups - 1, now_ref[rows - WIDTH + layer], 0.0
            )
    if len(edge_refs) == 1:
        at_top = lax.axis_index("depth") == 0
        for row in range(rows):
            edge_refs[0][row] = jnp.where(
                at_top, now_ref[row, depth - WIDTH :], now_ref[row, :WIDTH]
            )
    elif edge_refs:
        for row in range(rows):
            edge_refs[0][row] = now_ref[row, depth - WIDTH :]
            edge_refs[1][row] = now_ref[row, :WIDTH]


def source_of(image, offset_of, background, now, earlier, step, groups, half_span, edges):
    rows, depth, width = background.shape
    extra = WIDTH * ((step == 1) + (step == groups - 1))
    return pl.pallas_call(
        functools.partial(source_kernel, half_span, step, groups),
        out_shape=[pltpu.VMEM((rows + extra, depth, width), jnp.float32)]
        + [pltpu.VMEM((rows, WIDTH, width), now.dtype)] * edges,
        in_specs=[SMEM, VMEM, VMEM, VMEM, ANY],
        out_specs=[VMEM] * (1 + edges),
        compiler_params=pltpu.CompilerParams(vmem_limit_bytes=32 * MIB),
        cost_estimate=COST,
    )(offset_of, image, background, now, earlier)


def step_kernel(half_span, offset_ref, image_ref, background_ref, now_ref, above_ref, below_ref, prev_ref, courant_ref, out_ref, deep_ref):
    rows, depth, width = now_ref.shape
    at = lax.axis_index("depth")
    deep_ref[:, 2 * WIDTH : 2 * WIDTH + depth] = now_ref[...]
    deep_ref[:, WIDTH : 2 * WIDTH] = jnp.where(
        at != 0, above_ref[...], 0.0
    )
    deep_ref[:, 2 * WIDTH + depth : 3 * WIDTH + depth] = jnp.where(
        at != lax.axis_size("depth") - 1, below_ref[...], 0.0
    )
    lane = lax.broadcasted_iota(jnp.int32, (depth, width), 1)
    own = slab_sums(half_span, offset_ref, image_ref, background_ref, lax.axis_index("off"))
    for row in range(rows):
        centre = now_ref[row]
        bending = 3.0 * STENCIL[0] * centre
        for radius in range(1, WIDTH + 1):
            beside = deep_ref[row, 2 * WIDTH - radius : 2 * WIDTH - radius + depth]
            beside = beside + deep_ref[row, 2 * WIDTH + radius : 2 * WIDTH + radius + depth]
            if row >= radius:
                beside = beside + now_ref[row - radius]
            if row + radius < rows:
                beside = beside + now_ref[row + radius]
            left = jnp.where(lane >= radius, pltpu.roll(centre, radius, 1), 0.0)
            right = jnp.where(lane < width - radius, pltpu.roll(centre, width - radius, 1), 0.0)
            bending = bending + STENCIL[radius] * (beside + (left + right))
        out_ref[row] = 2.0 * centre - prev_ref[row] + courant_ref[row] * (bending + own[row])


def deep_layers(edges):
    count = lax.axis_size("depth")
    if count == 2:
        other = lax.ppermute(edges[0], "depth", [(0, 1), (1, 0)])
        return other, other
    return (
        lax.ppermute(edges[0], "depth", [(i, i + 1) for i in range(count - 1)]),
        lax.ppermute(edges[1], "depth", [(i + 1, i) for i in range(count - 1)]),
    )


def on_device(half_span, image, offset_of, background, wave_now, wave_prev, courant):
    groups = lax.axis_size("off")
    own_slab, prev = background[0], wave_prev[0]

    slabs = {}
    order = sorted(range(1, groups), key=lambda step: min(step, groups - step))
    for step in order:
        slabs[step] = lax.ppermute(
            own_slab, "off", [(i, (i + step) % groups) for i in range(groups)]
        )
    held, now, cells, own_slab = moved(
        (image, pltpu.VMEM),
        (wave_now[0], pltpu.VMEM),
        (offset_of, pltpu.SMEM),
        (own_slab, pltpu.VMEM),
    )
    rows, depth, width = now.shape

    returned = {}
    part = now
    for step in order:
        edges = 0 if step != order[0] else 1 if lax.axis_size("depth") == 2 else 2
        part, *rest = source_of(
            held, cells, slabs[step], now, part, step, groups, half_span, edges
        )
        if edges:
            above, below = deep_layers(rest)
        back = [(i, (i - step) % groups) for i in range(groups)]
        returned[step] = lax.ppermute(part.astype(jnp.float16), "off", back).astype(jnp.float32)
    returned = [returned[step] for step in range(1, groups)]

    base = pl.pallas_call(
        functools.partial(step_kernel, half_span),
        out_shape=jax.ShapeDtypeStruct(now.shape, jnp.float32),
        in_specs=[SMEM] + [VMEM] * 7,
        out_specs=VMEM,
        scratch_shapes=[pltpu.VMEM((rows, depth + 4 * WIDTH, width), jnp.float32)],
        compiler_params=pltpu.CompilerParams(vmem_limit_bytes=32 * MIB),
        cost_estimate=COST,
    )(cells, held, own_slab, now, above, below, prev, courant)

    after, before = returned[0][rows : rows + WIDTH], returned[-1][-WIDTH:]
    beside = jnp.concatenate([before, jnp.zeros_like(now), after], axis=0)
    sums = functools.reduce(jnp.add, [part[:rows] for part in returned])
    for radius in range(1, WIDTH + 1):
        sums = sums + STENCIL[radius] * (
            beside[WIDTH - radius : WIDTH - radius + rows]
            + beside[WIDTH + radius : WIDTH + radius + rows]
        )
    return (base + courant * sums)[None]


def solution(mesh):
    def whole(image, offset_of, background, wave_now, wave_prev, courant):
        half_span = offset_of.shape[0] // 2
        assert half_span < LANES and background.shape[-1] % LANES == 0
        return jax.shard_map(
            functools.partial(on_device, half_span),
            mesh=mesh,
            in_specs=(
                P("off", None, "depth", None),
                P("off"),
                P(("parts", "shot"), "off", "depth", None),
                P(("parts", "shot"), "off", "depth", None),
                P(("parts", "shot"), "off", "depth", None),
                P("off", "depth", None),
            ),
            out_specs=P(("parts", "shot"), "off", "depth", None),
            check_vma=False,
        )(image, offset_of, background, wave_now, wave_prev, courant)

    return whole
```

```python
import functools

import jax
import jax.numpy as jnp
from jax import lax
from jax.experimental import pallas as pl
from jax.experimental.pallas import tpu as pltpu
from jax.sharding import PartitionSpec as P

STENCIL = (-205.0 / 72.0, 8.0 / 5.0, -1.0 / 5.0, 8.0 / 315.0, -1.0 / 560.0)
WIDTH = len(STENCIL) - 1
LANES = 128
MIB = 2**20

VMEM = pl.BlockSpec(memory_space=pltpu.VMEM)
SMEM = pl.BlockSpec(memory_space=pltpu.SMEM)
ANY = pl.BlockSpec(memory_space=pl.ANY)
COST = pl.CostEstimate(flops=1000, bytes_accessed=1000, transcendentals=0)


def add_column(half_span, offset_ref, image_ref, background_ref, first_row, column, running):
    rows, depth, width = background_ref.shape
    cells = offset_ref[column] - half_span
    back = cells < 0
    turn = jnp.where(back, cells + LANES, cells)
    wrapped = lax.broadcasted_iota(jnp.int32, (depth, LANES), 1) < turn
    result = []
    for row in range(rows):
        turned = [
            pltpu.roll(background_ref[row, :, start : start + LANES], turn, 1)
            for start in range(0, width, LANES)
        ]
        zero = jnp.zeros_like(turned[0])
        ahead = [zero] + turned
        behind = turned + [zero]
        chosen = [jnp.where(back, b, a) for a, b in zip(ahead, behind)]
        shifted = [jnp.where(wrapped, a, b) for a, b in zip(chosen[:-1], chosen[1:])]
        factor = image_ref[column, first_row + row].astype(jnp.float32)
        result.append(running[row] + factor * jnp.concatenate(shifted, 1).astype(jnp.float32))
    return tuple(result)


def slab_sums(half_span, offset_ref, image_ref, background_ref, slab):
    rows, depth, width = background_ref.shape
    add = functools.partial(
        add_column, half_span, offset_ref, image_ref, background_ref, slab * rows
    )
    totals = (jnp.zeros((depth, width), jnp.float32),) * rows
    for column in range(image_ref.shape[0]):
        totals = add(column, totals)
    return totals


def move_kernel(*refs):
    count = (len(refs) - 1) // 2
    arrived = refs[-1]
    copies = [
        pltpu.make_async_copy(refs[i], refs[count + i], arrived.at[i]) for i in range(count)
    ]
    for copy in copies:
        copy.start()
    for copy in copies:
        copy.wait()


BALANCE = 313


def moved(beside, *pairs):
    return pl.pallas_call(
        move_kernel,
        out_shape=[space(x.shape, x.dtype) for x, space in pairs],
        in_specs=[ANY] * len(pairs),
        out_specs=[pl.BlockSpec(memory_space=space) for _, space in pairs],
        scratch_shapes=[pltpu.SemaphoreType.DMA((len(pairs),))],
        compiler_params=pltpu.CompilerParams(vmem_limit_bytes=32 * MIB),
        cost_estimate=pl.CostEstimate(flops=BALANCE * beside.size * beside.dtype.itemsize, bytes_accessed=0, transcendentals=0),
    )(*[pltpu.with_memory_space_constraint(x, pltpu.HBM) for x, _ in pairs])


def source_kernel(half_span, step, groups, offset_ref, image_ref, background_ref, now_ref, earlier_ref, out_ref, *edge_refs):
    del earlier_ref
    rows, depth, width = background_ref.shape
    here = lax.axis_index("off")
    slab = lax.rem(here - step + groups, groups)
    totals = slab_sums(half_span, offset_ref, image_ref, background_ref, slab)
    for row in range(rows):
        out_ref[row] = totals[row]
    at = rows
    if step == 1:
        for layer in range(WIDTH):
            out_ref[at + layer] = jnp.where(here != 0, now_ref[layer], 0.0)
        at += WIDTH
    if step == groups - 1:
        for layer in range(WIDTH):
            out_ref[at + layer] = jnp.where(
                here != groups - 1, now_ref[rows - WIDTH + layer], 0.0
            )
        at += WIDTH
    for rest in range(at, out_ref.shape[0]):
        out_ref[rest] = jnp.zeros((depth, width), jnp.float32)
    if len(edge_refs) == 1:
        at_top = lax.axis_index("depth") == 0
        for row in range(rows):
            edge_refs[0][row] = jnp.where(
                at_top, now_ref[row, depth - WIDTH :], now_ref[row, :WIDTH]
            )
    elif edge_refs:
        for row in range(rows):
            edge_refs[0][row] = now_ref[row, depth - WIDTH :]
            edge_refs[1][row] = now_ref[row, :WIDTH]


def source_of(image, offset_of, background, now, earlier, step, groups, half_span, edges):
    rows, depth, width = background.shape
    extra = WIDTH * ((step == 1) + (step == groups - 1)) + (edges > 0)
    return pl.pallas_call(
        functools.partial(source_kernel, half_span, step, groups),
        out_shape=[pltpu.VMEM((rows + extra, depth, width), jnp.float32)]
        + [pltpu.VMEM((rows, WIDTH, width), now.dtype)] * edges,
        in_specs=[SMEM, VMEM, VMEM, VMEM, ANY],
        out_specs=[VMEM] * (1 + edges),
        compiler_params=pltpu.CompilerParams(vmem_limit_bytes=32 * MIB),
        cost_estimate=COST,
    )(offset_of, image, background, now, earlier)


def step_kernel(half_span, offset_ref, image_ref, background_ref, now_ref, prev_ref, courant_ref, out_ref, deep_ref):
    rows, depth, width = now_ref.shape
    deep_ref[:, 2 * WIDTH : 2 * WIDTH + depth] = now_ref[...]
    deep_ref[:, WIDTH : 2 * WIDTH] = jnp.zeros((rows, WIDTH, width), jnp.float32)
    deep_ref[:, 2 * WIDTH + depth : 3 * WIDTH + depth] = jnp.zeros(
        (rows, WIDTH, width), jnp.float32
    )
    lane = lax.broadcasted_iota(jnp.int32, (depth, width), 1)
    own = slab_sums(half_span, offset_ref, image_ref, background_ref, lax.axis_index("off"))
    for row in range(rows):
        centre = now_ref[row]
        bending = 3.0 * STENCIL[0] * centre
        for radius in range(1, WIDTH + 1):
            beside = deep_ref[row, 2 * WIDTH - radius : 2 * WIDTH - radius + depth]
            beside = beside + deep_ref[row, 2 * WIDTH + radius : 2 * WIDTH + radius + depth]
            if row >= radius:
                beside = beside + now_ref[row - radius]
            if row + radius < rows:
                beside = beside + now_ref[row + radius]
            left = jnp.where(lane >= radius, pltpu.roll(centre, radius, 1), 0.0)
            right = jnp.where(lane < width - radius, pltpu.roll(centre, width - radius, 1), 0.0)
            bending = bending + STENCIL[radius] * (beside + (left + right))
        out_ref[row] = 2.0 * centre - prev_ref[row] + courant_ref[row] * (bending + own[row])


def deep_kernel(base_ref, above_ref, below_ref, courant_ref, out_ref):
    rows, depth, width = base_ref.shape
    at = lax.axis_index("depth")
    inside_above = (at != 0).astype(jnp.float32)
    inside_below = (at != lax.axis_size("depth") - 1).astype(jnp.float32)
    gap = jnp.zeros((depth - 2 * WIDTH, width), jnp.float32)
    for row in range(rows):
        above = above_ref[row] * inside_above
        below = below_ref[row] * inside_below
        upper, lower = [], []
        for layer in range(WIDTH):
            upper.append(
                sum(
                    STENCIL[radius] * above[WIDTH + layer - radius : WIDTH + layer - radius + 1]
                    for radius in range(layer + 1, WIDTH + 1)
                )
            )
            lower.append(
                sum(
                    STENCIL[radius] * below[layer + radius - WIDTH : layer + radius - WIDTH + 1]
                    for radius in range(WIDTH - layer, WIDTH + 1)
                )
            )
        bending = jnp.concatenate(upper + [gap] + lower, axis=0)
        out_ref[row] = base_ref[row] + courant_ref[row] * bending


def deep_layers(edges):
    count = lax.axis_size("depth")
    if count == 2:
        other = lax.ppermute(edges[0], "depth", [(0, 1), (1, 0)])
        return other, other
    return (
        lax.ppermute(edges[0], "depth", [(i, i + 1) for i in range(count - 1)]),
        lax.ppermute(edges[1], "depth", [(i + 1, i) for i in range(count - 1)]),
    )


def on_device(half_span, image, offset_of, background, wave_now, wave_prev, courant):
    groups = lax.axis_size("off")
    own_slab, prev = background[0], wave_prev[0]

    slabs = {}
    order = sorted(range(1, groups), key=lambda step: min(step, groups - step))
    for step in order:
        slabs[step] = lax.ppermute(
            own_slab, "off", [(i, (i + step) % groups) for i in range(groups)]
        )
    held = pltpu.with_memory_space_constraint(image, pltpu.VMEM)
    now, cells, own_slab = moved(
        image,
        (wave_now[0], pltpu.VMEM),
        (offset_of, pltpu.SMEM),
        (own_slab, pltpu.VMEM),
    )
    rows, depth, width = now.shape

    returned = {}
    part = now
    for step in order:
        edges = 0 if step != order[0] else 1 if lax.axis_size("depth") == 2 else 2
        part, *rest = source_of(
            held, cells, slabs[step], now, part, step, groups, half_span, edges
        )
        if edges:
            above, below = deep_layers(rest)
        back = [(i, (i - step) % groups) for i in range(groups)]
        returned[step] = lax.ppermute(part.astype(jnp.float16), "off", back).astype(jnp.float32)
    returned = [returned[step] for step in range(1, groups)]

    base = pl.pallas_call(
        functools.partial(step_kernel, half_span),
        out_shape=pltpu.VMEM(now.shape, jnp.float32),
        in_specs=[SMEM] + [VMEM] * 5,
        out_specs=VMEM,
        scratch_shapes=[pltpu.VMEM((rows, depth + 4 * WIDTH, width), jnp.float32)],
        compiler_params=pltpu.CompilerParams(vmem_limit_bytes=32 * MIB),
        cost_estimate=COST,
    )(cells, held, own_slab, now, prev, courant)
    base = pl.pallas_call(
        deep_kernel,
        out_shape=pltpu.VMEM(now.shape, jnp.float32),
        in_specs=[VMEM] * 4,
        out_specs=VMEM,
        compiler_params=pltpu.CompilerParams(vmem_limit_bytes=32 * MIB),
        cost_estimate=COST,
    )(base, above, below, courant)

    at = rows if groups > 2 else rows + WIDTH
    after, before = returned[0][rows : rows + WIDTH], returned[-1][at : at + WIDTH]
    beside = jnp.concatenate([before, jnp.zeros_like(now), after], axis=0)
    sums = functools.reduce(jnp.add, [part[:rows] for part in returned])
    for radius in range(1, WIDTH + 1):
        sums = sums + STENCIL[radius] * (
            beside[WIDTH - radius : WIDTH - radius + rows]
            + beside[WIDTH + radius : WIDTH + radius + rows]
        )
    return (base + courant * sums)[None]


def solution(mesh):
    def whole(image, offset_of, background, wave_now, wave_prev, courant):
        half_span = offset_of.shape[0] // 2
        assert half_span < LANES and background.shape[-1] % LANES == 0
        return jax.shard_map(
            functools.partial(on_device, half_span),
            mesh=mesh,
            in_specs=(
                P("off", None, "depth", None),
                P("off"),
                P(("parts", "shot"), "off", "depth", None),
                P(("parts", "shot"), "off", "depth", None),
                P(("parts", "shot"), "off", "depth", None),
                P("off", "depth", None),
            ),
            out_specs=P(("parts", "shot"), "off", "depth", None),
            check_vma=False,
        )(image, offset_of, background, wave_now, wave_prev, courant)

    return whole
```

```python
import functools

import jax
import jax.numpy as jnp
from jax import lax
from jax.experimental import pallas as pl
from jax.experimental.pallas import tpu as pltpu
from jax.sharding import PartitionSpec as P

STENCIL = (-205.0 / 72.0, 8.0 / 5.0, -1.0 / 5.0, 8.0 / 315.0, -1.0 / 560.0)
WIDTH = len(STENCIL) - 1
LANES = 128
MIB = 2**20

VMEM = pl.BlockSpec(memory_space=pltpu.VMEM)
SMEM = pl.BlockSpec(memory_space=pltpu.SMEM)
ANY = pl.BlockSpec(memory_space=pl.ANY)
COST = pl.CostEstimate(flops=1000, bytes_accessed=1000, transcendentals=0)


def add_column(half_span, offset_ref, image_ref, background_ref, first_row, column, running):
    rows, depth, width = background_ref.shape
    cells = offset_ref[column] - half_span
    back = cells < 0
    turn = jnp.where(back, cells + LANES, cells)
    wrapped = lax.broadcasted_iota(jnp.int32, (depth, LANES), 1) < turn
    result = []
    for row in range(rows):
        turned = [
            pltpu.roll(background_ref[row, :, start : start + LANES], turn, 1)
            for start in range(0, width, LANES)
        ]
        zero = jnp.zeros_like(turned[0])
        ahead = [zero] + turned
        behind = turned + [zero]
        chosen = [jnp.where(back, b, a) for a, b in zip(ahead, behind)]
        shifted = [jnp.where(wrapped, a, b) for a, b in zip(chosen[:-1], chosen[1:])]
        factor = image_ref[column, first_row + row].astype(jnp.float32)
        result.append(running[row] + factor * jnp.concatenate(shifted, 1).astype(jnp.float32))
    return tuple(result)


def slab_sums(half_span, offset_ref, image_ref, background_ref, slab):
    rows, depth, width = background_ref.shape
    add = functools.partial(
        add_column, half_span, offset_ref, image_ref, background_ref, slab * rows
    )
    totals = (jnp.zeros((depth, width), jnp.float32),) * rows
    for column in range(image_ref.shape[0]):
        totals = add(column, totals)
    return totals


def move_kernel(*refs):
    count = (len(refs) - 1) // 2
    arrived = refs[-1]
    copies = [
        pltpu.make_async_copy(refs[i], refs[count + i], arrived.at[i]) for i in range(count)
    ]
    for copy in copies:
        copy.start()
    for copy in copies:
        copy.wait()


SCALE = 64.0


def moved(beside, *pairs):
    return pl.pallas_call(
        move_kernel,
        out_shape=[space(x.shape, x.dtype) for x, space in pairs],
        in_specs=[ANY] * len(pairs),
        out_specs=[pl.BlockSpec(memory_space=space) for _, space in pairs],
        scratch_shapes=[pltpu.SemaphoreType.DMA((len(pairs),))],
        compiler_params=pltpu.CompilerParams(vmem_limit_bytes=32 * MIB),
        cost_estimate=pl.CostEstimate(flops=0, bytes_accessed=0, transcendentals=5 * beside.size // 3),
    )(*[pltpu.with_memory_space_constraint(x, pltpu.HBM) for x, _ in pairs])


def source_kernel(half_span, step, groups, offset_ref, image_ref, background_ref, now_ref, earlier_ref, out_ref, *edge_refs):
    del earlier_ref
    rows, depth, width = background_ref.shape
    here = lax.axis_index("off")
    slab = lax.rem(here - step + groups, groups)
    totals = slab_sums(half_span, offset_ref, image_ref, background_ref, slab)
    for row in range(rows):
        out_ref[row] = SCALE * totals[row]
    at = rows
    if step == 1:
        for layer in range(WIDTH):
            out_ref[at + layer] = jnp.where(here != 0, SCALE * now_ref[layer], 0.0)
        at += WIDTH
    if step == groups - 1:
        for layer in range(WIDTH):
            out_ref[at + layer] = jnp.where(
                here != groups - 1, SCALE * now_ref[rows - WIDTH + layer], 0.0
            )
    if len(edge_refs) == 1:
        at_top = lax.axis_index("depth") == 0
        for row in range(rows):
            edge_refs[0][row] = jnp.where(
                at_top, now_ref[row, depth - WIDTH :], now_ref[row, :WIDTH]
            )
    elif edge_refs:
        for row in range(rows):
            edge_refs[0][row] = now_ref[row, depth - WIDTH :]
            edge_refs[1][row] = now_ref[row, :WIDTH]


def source_of(image, offset_of, background, now, earlier, step, groups, half_span, edges):
    rows, depth, width = background.shape
    extra = WIDTH * ((step == 1) + (step == groups - 1))
    return pl.pallas_call(
        functools.partial(source_kernel, half_span, step, groups),
        out_shape=[pltpu.VMEM((rows + extra, depth, width), jnp.float32)]
        + [pltpu.VMEM((rows, WIDTH, width), now.dtype)] * edges,
        in_specs=[SMEM, VMEM, VMEM, VMEM, ANY],
        out_specs=[VMEM] * (1 + edges),
        compiler_params=pltpu.CompilerParams(vmem_limit_bytes=32 * MIB),
        cost_estimate=COST,
    )(offset_of, image, background, now, earlier)


def step_kernel(half_span, offset_ref, image_ref, background_ref, now_ref, prev_ref, courant_ref, out_ref, deep_ref):
    rows, depth, width = now_ref.shape
    deep_ref[:, 2 * WIDTH : 2 * WIDTH + depth] = now_ref[...]
    deep_ref[:, WIDTH : 2 * WIDTH] = jnp.zeros((rows, WIDTH, width), jnp.float32)
    deep_ref[:, 2 * WIDTH + depth : 3 * WIDTH + depth] = jnp.zeros(
        (rows, WIDTH, width), jnp.float32
    )
    lane = lax.broadcasted_iota(jnp.int32, (depth, width), 1)
    own = slab_sums(half_span, offset_ref, image_ref, background_ref, lax.axis_index("off"))
    for row in range(rows):
        centre = now_ref[row]
        bending = 3.0 * STENCIL[0] * centre
        for radius in range(1, WIDTH + 1):
            beside = deep_ref[row, 2 * WIDTH - radius : 2 * WIDTH - radius + depth]
            beside = beside + deep_ref[row, 2 * WIDTH + radius : 2 * WIDTH + radius + depth]
            if row >= radius:
                beside = beside + now_ref[row - radius]
            if row + radius < rows:
                beside = beside + now_ref[row + radius]
            left = jnp.where(lane >= radius, pltpu.roll(centre, radius, 1), 0.0)
            right = jnp.where(lane < width - radius, pltpu.roll(centre, width - radius, 1), 0.0)
            bending = bending + STENCIL[radius] * (beside + (left + right))
        out_ref[row] = 2.0 * centre - prev_ref[row] + courant_ref[row] * (bending + own[row])


def deep_kernel(base_ref, above_ref, below_ref, courant_ref, out_ref):
    rows, depth, width = base_ref.shape
    at = lax.axis_index("depth")
    inside_above = (at != 0).astype(jnp.float32)
    inside_below = (at != lax.axis_size("depth") - 1).astype(jnp.float32)
    gap = jnp.zeros((depth - 2 * WIDTH, width), jnp.float32)
    for row in range(rows):
        above = above_ref[row] * inside_above
        below = below_ref[row] * inside_below
        upper, lower = [], []
        for layer in range(WIDTH):
            upper.append(
                sum(
                    STENCIL[radius] * above[WIDTH + layer - radius : WIDTH + layer - radius + 1]
                    for radius in range(layer + 1, WIDTH + 1)
                )
            )
            lower.append(
                sum(
                    STENCIL[radius] * below[layer + radius - WIDTH : layer + radius - WIDTH + 1]
                    for radius in range(WIDTH - layer, WIDTH + 1)
                )
            )
        bending = jnp.concatenate(upper + [gap] + lower, axis=0)
        out_ref[row] = base_ref[row] + courant_ref[row] * bending


def deep_layers(edges):
    count = lax.axis_size("depth")
    if count == 2:
        other = lax.ppermute(edges[0], "depth", [(0, 1), (1, 0)])
        return other, other
    return (
        lax.ppermute(edges[0], "depth", [(i, i + 1) for i in range(count - 1)]),
        lax.ppermute(edges[1], "depth", [(i + 1, i) for i in range(count - 1)]),
    )


def on_device(half_span, image, offset_of, background, wave_now, wave_prev, courant):
    groups = lax.axis_size("off")
    own_slab, prev = background[0], wave_prev[0]

    slabs = {}
    order = sorted(range(1, groups), key=lambda step: min(step, groups - step))
    for step in order:
        slabs[step] = lax.ppermute(
            own_slab, "off", [(i, (i + step) % groups) for i in range(groups)]
        )
    held = pltpu.with_memory_space_constraint(image, pltpu.VMEM)
    now, cells, own_slab = moved(
        image,
        (wave_now[0], pltpu.VMEM),
        (offset_of, pltpu.SMEM),
        (own_slab, pltpu.VMEM),
    )
    rows, depth, width = now.shape

    returned = {}
    part = now
    for step in order:
        edges = 0 if step != order[0] else 1 if lax.axis_size("depth") == 2 else 2
        part, *rest = source_of(
            held, cells, slabs[step], now, part, step, groups, half_span, edges
        )
        if edges:
            above, below = deep_layers(rest)
        back = [(i, (i - step) % groups) for i in range(groups)]
        returned[step] = lax.ppermute(part.astype(jnp.float16), "off", back).astype(jnp.float32)
    returned = [returned[step] for step in range(1, groups)]

    base = pl.pallas_call(
        functools.partial(step_kernel, half_span),
        out_shape=pltpu.VMEM(now.shape, jnp.float32),
        in_specs=[SMEM] + [VMEM] * 5,
        out_specs=VMEM,
        scratch_shapes=[pltpu.VMEM((rows, depth + 4 * WIDTH, width), jnp.float32)],
        compiler_params=pltpu.CompilerParams(vmem_limit_bytes=32 * MIB),
        cost_estimate=COST,
    )(cells, held, own_slab, now, prev, courant)
    base = pl.pallas_call(
        deep_kernel,
        out_shape=pltpu.VMEM(now.shape, jnp.float32),
        in_specs=[VMEM] * 4,
        out_specs=VMEM,
        compiler_params=pltpu.CompilerParams(vmem_limit_bytes=32 * MIB),
        cost_estimate=COST,
    )(base, above, below, courant)

    at = rows if groups > 2 else rows + WIDTH
    after, before = returned[0][rows : rows + WIDTH], returned[-1][at : at + WIDTH]
    beside = jnp.concatenate([before, jnp.zeros_like(now), after], axis=0)
    sums = functools.reduce(jnp.add, [part[:rows] for part in reversed(returned)])
    for radius in range(1, WIDTH + 1):
        sums = sums + STENCIL[radius] * (
            beside[WIDTH - radius : WIDTH - radius + rows]
            + beside[WIDTH + radius : WIDTH + radius + rows]
        )
    return (base + courant * (sums * (1.0 / SCALE)))[None]


def solution(mesh):
    def whole(image, offset_of, background, wave_now, wave_prev, courant):
        half_span = offset_of.shape[0] // 2
        assert half_span < LANES and background.shape[-1] % LANES == 0
        return jax.shard_map(
            functools.partial(on_device, half_span),
            mesh=mesh,
            in_specs=(
                P("off", None, "depth", None),
                P("off"),
                P(("parts", "shot"), "off", "depth", None),
                P(("parts", "shot"), "off", "depth", None),
                P(("parts", "shot"), "off", "depth", None),
                P("off", "depth", None),
            ),
            out_specs=P(("parts", "shot"), "off", "depth", None),
            check_vma=False,
        )(image, offset_of, background, wave_now, wave_prev, courant)

    return whole
```

```python
import functools

import jax
import jax.numpy as jnp
from jax import lax
from jax.experimental import pallas as pl
from jax.experimental.pallas import tpu as pltpu
from jax.sharding import PartitionSpec as P

STENCIL = (-205.0 / 72.0, 8.0 / 5.0, -1.0 / 5.0, 8.0 / 315.0, -1.0 / 560.0)
WIDTH = len(STENCIL) - 1
LANES = 128
MIB = 2**20

VMEM = pl.BlockSpec(memory_space=pltpu.VMEM)
SMEM = pl.BlockSpec(memory_space=pltpu.SMEM)
ANY = pl.BlockSpec(memory_space=pl.ANY)
COST = pl.CostEstimate(flops=1000, bytes_accessed=1000, transcendentals=0)


def add_column(half_span, offset_ref, image_ref, background_ref, first_row, column, running):
    rows, depth, width = background_ref.shape
    cells = offset_ref[column] - half_span
    back = cells < 0
    turn = jnp.where(back, cells + LANES, cells)
    wrapped = lax.broadcasted_iota(jnp.int32, (depth, LANES), 1) < turn
    result = []
    for row in range(rows):
        turned = [
            pltpu.roll(background_ref[row, :, start : start + LANES], turn, 1)
            for start in range(0, width, LANES)
        ]
        zero = jnp.zeros_like(turned[0])
        ahead = [zero] + turned
        behind = turned + [zero]
        chosen = [jnp.where(back, b, a) for a, b in zip(ahead, behind)]
        shifted = [jnp.where(wrapped, a, b) for a, b in zip(chosen[:-1], chosen[1:])]
        factor = image_ref[column, first_row + row].astype(jnp.float32)
        result.append(running[row] + factor * jnp.concatenate(shifted, 1).astype(jnp.float32))
    return tuple(result)


def slab_sums(half_span, offset_ref, image_ref, background_ref, slab):
    rows, depth, width = background_ref.shape
    add = functools.partial(
        add_column, half_span, offset_ref, image_ref, background_ref, slab * rows
    )
    totals = (jnp.zeros((depth, width), jnp.float32),) * rows
    for column in range(image_ref.shape[0]):
        totals = add(column, totals)
    return totals


def move_kernel(*refs):
    count = (len(refs) - 1) // 2
    arrived = refs[-1]
    copies = [
        pltpu.make_async_copy(refs[i], refs[count + i], arrived.at[i]) for i in range(count)
    ]
    for copy in copies:
        copy.start()
    for copy in copies:
        copy.wait()


SCALE = 64.0


def moved(beside, *pairs):
    return pl.pallas_call(
        move_kernel,
        out_shape=[space(x.shape, x.dtype) for x, space in pairs],
        in_specs=[ANY] * len(pairs),
        out_specs=[pl.BlockSpec(memory_space=space) for _, space in pairs],
        scratch_shapes=[pltpu.SemaphoreType.DMA((len(pairs),))],
        compiler_params=pltpu.CompilerParams(vmem_limit_bytes=32 * MIB),
        cost_estimate=pl.CostEstimate(flops=0, bytes_accessed=0, transcendentals=5 * beside.size // 3),
    )(*[pltpu.with_memory_space_constraint(x, pltpu.HBM) for x, _ in pairs])


def source_kernel(half_span, step, groups, offset_ref, image_ref, background_ref, now_ref, earlier_ref, out_ref, *edge_refs):
    del earlier_ref
    rows, depth, width = background_ref.shape
    here = lax.axis_index("off")
    slab = lax.rem(here - step + groups, groups)
    totals = slab_sums(half_span, offset_ref, image_ref, background_ref, slab)
    for row in range(rows):
        out_ref[row] = SCALE * totals[row]
    at = rows
    if step == 1:
        for layer in range(WIDTH):
            out_ref[at + layer] = jnp.where(here != 0, SCALE * now_ref[layer], 0.0)
        at += WIDTH
    if step == groups - 1:
        for layer in range(WIDTH):
            out_ref[at + layer] = jnp.where(
                here != groups - 1, SCALE * now_ref[rows - WIDTH + layer], 0.0
            )
    if len(edge_refs) == 1:
        at_top = lax.axis_index("depth") == 0
        for row in range(rows):
            edge_refs[0][row] = jnp.where(
                at_top, now_ref[row, depth - WIDTH :], now_ref[row, :WIDTH]
            )
    elif edge_refs:
        for row in range(rows):
            edge_refs[0][row] = now_ref[row, depth - WIDTH :]
            edge_refs[1][row] = now_ref[row, :WIDTH]


def source_of(image, offset_of, background, now, earlier, step, groups, half_span, edges):
    rows, depth, width = background.shape
    extra = WIDTH * ((step == 1) + (step == groups - 1))
    return pl.pallas_call(
        functools.partial(source_kernel, half_span, step, groups),
        out_shape=[pltpu.VMEM((rows + extra, depth, width), jnp.float32)]
        + [pltpu.VMEM((rows, WIDTH, width), now.dtype)] * edges,
        in_specs=[SMEM, VMEM, VMEM, VMEM, ANY],
        out_specs=[VMEM] * (1 + edges),
        compiler_params=pltpu.CompilerParams(vmem_limit_bytes=32 * MIB),
        cost_estimate=COST,
    )(offset_of, image, background, now, earlier)


def step_kernel(half_span, offset_ref, image_ref, background_ref, now_ref, prev_ref, courant_ref, out_ref, deep_ref):
    rows, depth, width = now_ref.shape
    deep_ref[:, 2 * WIDTH : 2 * WIDTH + depth] = now_ref[...]
    deep_ref[:, WIDTH : 2 * WIDTH] = jnp.zeros((rows, WIDTH, width), jnp.float32)
    deep_ref[:, 2 * WIDTH + depth : 3 * WIDTH + depth] = jnp.zeros(
        (rows, WIDTH, width), jnp.float32
    )
    lane = lax.broadcasted_iota(jnp.int32, (depth, width), 1)
    own = slab_sums(half_span, offset_ref, image_ref, background_ref, lax.axis_index("off"))
    for row in range(rows):
        centre = now_ref[row]
        bending = 3.0 * STENCIL[0] * centre
        for radius in range(1, WIDTH + 1):
            beside = deep_ref[row, 2 * WIDTH - radius : 2 * WIDTH - radius + depth]
            beside = beside + deep_ref[row, 2 * WIDTH + radius : 2 * WIDTH + radius + depth]
            if row >= radius:
                beside = beside + now_ref[row - radius]
            if row + radius < rows:
                beside = beside + now_ref[row + radius]
            left = jnp.where(lane >= radius, pltpu.roll(centre, radius, 1), 0.0)
            right = jnp.where(lane < width - radius, pltpu.roll(centre, width - radius, 1), 0.0)
            bending = bending + STENCIL[radius] * (beside + (left + right))
        out_ref[row] = 2.0 * centre - prev_ref[row] + courant_ref[row] * (bending + own[row])


def deep_kernel(base_ref, above_ref, below_ref, courant_ref, out_ref):
    rows, depth, width = base_ref.shape
    at = lax.axis_index("depth")
    inside_above = (at != 0).astype(jnp.float32)
    inside_below = (at != lax.axis_size("depth") - 1).astype(jnp.float32)
    gap = jnp.zeros((depth - 2 * WIDTH, width), jnp.float32)
    for row in range(rows):
        above = above_ref[row] * inside_above
        below = below_ref[row] * inside_below
        upper, lower = [], []
        for layer in range(WIDTH):
            upper.append(
                sum(
                    STENCIL[radius] * above[WIDTH + layer - radius : WIDTH + layer - radius + 1]
                    for radius in range(layer + 1, WIDTH + 1)
                )
            )
            lower.append(
                sum(
                    STENCIL[radius] * below[layer + radius - WIDTH : layer + radius - WIDTH + 1]
                    for radius in range(WIDTH - layer, WIDTH + 1)
                )
            )
        bending = jnp.concatenate(upper + [gap] + lower, axis=0)
        out_ref[row] = base_ref[row] + courant_ref[row] * bending


def deep_layers(edges):
    count = lax.axis_size("depth")
    if count == 2:
        other = lax.ppermute(edges[0], "depth", [(0, 1), (1, 0)])
        return other, other
    return (
        lax.ppermute(edges[0], "depth", [(i, i + 1) for i in range(count - 1)]),
        lax.ppermute(edges[1], "depth", [(i + 1, i) for i in range(count - 1)]),
    )


def on_device(half_span, image, offset_of, background, wave_now, wave_prev, courant):
    groups = lax.axis_size("off")
    own_slab, prev = background[0], wave_prev[0]

    slabs = {}
    order = sorted(range(1, groups), key=lambda step: min(step, groups - step))
    for step in order:
        slabs[step] = lax.ppermute(
            own_slab, "off", [(i, (i + step) % groups) for i in range(groups)]
        )
    held = pltpu.with_memory_space_constraint(image, pltpu.VMEM)
    now, cells, own_slab = moved(
        image,
        (wave_now[0], pltpu.VMEM),
        (offset_of, pltpu.SMEM),
        (own_slab, pltpu.VMEM),
    )
    rows, depth, width = now.shape

    returned = {}
    part = now
    for step in order:
        edges = 0 if step != order[0] else 1 if lax.axis_size("depth") == 2 else 2
        part, *rest = source_of(
            held, cells, slabs[step], now, part, step, groups, half_span, edges
        )
        if edges:
            above, below = deep_layers(rest)
        back = [(i, (i - step) % groups) for i in range(groups)]
        returned[step] = lax.ppermute(part.astype(jnp.float16), "off", back).astype(jnp.float32)
    returned = [returned[step] for step in range(1, groups)]

    base = pl.pallas_call(
        functools.partial(step_kernel, half_span),
        out_shape=pltpu.VMEM(now.shape, jnp.float32),
        in_specs=[SMEM] + [VMEM] * 5,
        out_specs=VMEM,
        scratch_shapes=[pltpu.VMEM((rows, depth + 4 * WIDTH, width), jnp.float32)],
        compiler_params=pltpu.CompilerParams(vmem_limit_bytes=32 * MIB),
        cost_estimate=COST,
    )(cells, held, own_slab, now, prev, courant)
    base = pl.pallas_call(
        deep_kernel,
        out_shape=pltpu.VMEM(now.shape, jnp.float32),
        in_specs=[VMEM] * 4,
        out_specs=VMEM,
        compiler_params=pltpu.CompilerParams(vmem_limit_bytes=32 * MIB),
        cost_estimate=COST,
    )(base, above, below, courant)

    at = rows if groups > 2 else rows + WIDTH
    after, before = returned[0][rows : rows + WIDTH], returned[-1][at : at + WIDTH]
    beside = jnp.pad(before, ((0, WIDTH + rows), (0, 0), (0, 0)))
    beside = beside + jnp.pad(after, ((WIDTH + rows, 0), (0, 0), (0, 0)))
    sums = functools.reduce(jnp.add, [returned[at][:rows] for at in range(-1, groups - 2)])
    for radius in range(1, WIDTH + 1):
        sums = sums + STENCIL[radius] * (
            beside[WIDTH - radius : WIDTH - radius + rows]
            + beside[WIDTH + radius : WIDTH + radius + rows]
        )
    return (base + courant * (sums * (1.0 / SCALE)))[None]


def solution(mesh):
    def whole(image, offset_of, background, wave_now, wave_prev, courant):
        half_span = offset_of.shape[0] // 2
        assert half_span < LANES and background.shape[-1] % LANES == 0
        return jax.shard_map(
            functools.partial(on_device, half_span),
            mesh=mesh,
            in_specs=(
                P("off", None, "depth", None),
                P("off"),
                P(("parts", "shot"), "off", "depth", None),
                P(("parts", "shot"), "off", "depth", None),
                P(("parts", "shot"), "off", "depth", None),
                P("off", "depth", None),
            ),
            out_specs=P(("parts", "shot"), "off", "depth", None),
            check_vma=False,
        )(image, offset_of, background, wave_now, wave_prev, courant)

    return whole
```

```python
import functools

import jax
import jax.numpy as jnp
from jax import lax
from jax.experimental import pallas as pl
from jax.experimental.pallas import tpu as pltpu
from jax.sharding import PartitionSpec as P

STENCIL = (-205.0 / 72.0, 8.0 / 5.0, -1.0 / 5.0, 8.0 / 315.0, -1.0 / 560.0)
WIDTH = len(STENCIL) - 1
LANES = 128
MIB = 2**20

VMEM = pl.BlockSpec(memory_space=pltpu.VMEM)
SMEM = pl.BlockSpec(memory_space=pltpu.SMEM)
ANY = pl.BlockSpec(memory_space=pl.ANY)
COST = pl.CostEstimate(flops=1000, bytes_accessed=1000, transcendentals=0)


def add_column(half_span, offset_ref, image_ref, background_ref, first_row, column, running):
    rows, depth, width = background_ref.shape
    cells = offset_ref[column] - half_span
    back = cells < 0
    turn = jnp.where(back, cells + LANES, cells)
    wrapped = lax.broadcasted_iota(jnp.int32, (depth, LANES), 1) < turn
    result = []
    for row in range(rows):
        turned = [
            pltpu.roll(background_ref[row, :, start : start + LANES], turn, 1)
            for start in range(0, width, LANES)
        ]
        zero = jnp.zeros_like(turned[0])
        ahead = [zero] + turned
        behind = turned + [zero]
        chosen = [jnp.where(back, b, a) for a, b in zip(ahead, behind)]
        shifted = [jnp.where(wrapped, a, b) for a, b in zip(chosen[:-1], chosen[1:])]
        factor = image_ref[column, first_row + row].astype(jnp.float32)
        result.append(running[row] + factor * jnp.concatenate(shifted, 1).astype(jnp.float32))
    return tuple(result)


def slab_sums(half_span, offset_ref, image_ref, background_ref, slab):
    rows, depth, width = background_ref.shape
    add = functools.partial(
        add_column, half_span, offset_ref, image_ref, background_ref, slab * rows
    )
    totals = (jnp.zeros((depth, width), jnp.float32),) * rows
    for column in range(image_ref.shape[0]):
        totals = add(column, totals)
    return totals


def move_kernel(*refs):
    count = (len(refs) - 1) // 2
    arrived = refs[-1]
    copies = [
        pltpu.make_async_copy(refs[i], refs[count + i], arrived.at[i]) for i in range(count)
    ]
    for copy in copies:
        copy.start()
    for copy in copies:
        copy.wait()


SCALE = 64.0


def moved(beside, *pairs):
    return pl.pallas_call(
        move_kernel,
        out_shape=[space(x.shape, x.dtype) for x, space in pairs],
        in_specs=[ANY] * len(pairs),
        out_specs=[pl.BlockSpec(memory_space=space) for _, space in pairs],
        scratch_shapes=[pltpu.SemaphoreType.DMA((len(pairs),))],
        compiler_params=pltpu.CompilerParams(vmem_limit_bytes=32 * MIB),
        cost_estimate=pl.CostEstimate(flops=0, bytes_accessed=0, transcendentals=5 * beside.size // 3),
    )(*[pltpu.with_memory_space_constraint(x, pltpu.HBM) for x, _ in pairs])


def source_kernel(half_span, step, groups, offset_ref, image_ref, background_ref, now_ref, earlier_ref, out_ref, *edge_refs):
    del earlier_ref
    rows, depth, width = background_ref.shape
    here = lax.axis_index("off")
    slab = lax.rem(here - step + groups, groups)
    totals = slab_sums(half_span, offset_ref, image_ref, background_ref, slab)
    for row in range(rows):
        out_ref[row] = SCALE * totals[row]
    at = rows
    if step == 1:
        for layer in range(WIDTH):
            out_ref[at + layer] = jnp.where(here != 0, SCALE * now_ref[layer], 0.0)
        at += WIDTH
    if step == groups - 1:
        for layer in range(WIDTH):
            out_ref[at + layer] = jnp.where(
                here != groups - 1, SCALE * now_ref[rows - WIDTH + layer], 0.0
            )
    if len(edge_refs) == 1:
        at_top = lax.axis_index("depth") == 0
        for row in range(rows):
            edge_refs[0][row] = jnp.where(
                at_top, now_ref[row, depth - WIDTH :], now_ref[row, :WIDTH]
            )
    elif edge_refs:
        for row in range(rows):
            edge_refs[0][row] = now_ref[row, depth - WIDTH :]
            edge_refs[1][row] = now_ref[row, :WIDTH]


def source_of(image, offset_of, background, now, earlier, step, groups, half_span, edges):
    rows, depth, width = background.shape
    extra = WIDTH * ((step == 1) + (step == groups - 1))
    return pl.pallas_call(
        functools.partial(source_kernel, half_span, step, groups),
        out_shape=[pltpu.VMEM((rows + extra, depth, width), jnp.float32)]
        + [pltpu.VMEM((rows, WIDTH, width), now.dtype)] * edges,
        in_specs=[SMEM, VMEM, VMEM, VMEM, ANY],
        out_specs=[VMEM] * (1 + edges),
        compiler_params=pltpu.CompilerParams(vmem_limit_bytes=32 * MIB),
        cost_estimate=COST,
    )(offset_of, image, background, now, earlier)


def step_kernel(half_span, offset_ref, image_ref, background_ref, now_ref, prev_ref, courant_ref, out_ref, deep_ref):
    rows, depth, width = now_ref.shape
    deep_ref[:, 2 * WIDTH : 2 * WIDTH + depth] = now_ref[...]
    deep_ref[:, WIDTH : 2 * WIDTH] = jnp.zeros((rows, WIDTH, width), jnp.float32)
    deep_ref[:, 2 * WIDTH + depth : 3 * WIDTH + depth] = jnp.zeros(
        (rows, WIDTH, width), jnp.float32
    )
    lane = lax.broadcasted_iota(jnp.int32, (depth, width), 1)
    own = slab_sums(half_span, offset_ref, image_ref, background_ref, lax.axis_index("off"))
    for row in range(rows):
        centre = now_ref[row]
        bending = 3.0 * STENCIL[0] * centre
        for radius in range(1, WIDTH + 1):
            beside = deep_ref[row, 2 * WIDTH - radius : 2 * WIDTH - radius + depth]
            beside = beside + deep_ref[row, 2 * WIDTH + radius : 2 * WIDTH + radius + depth]
            if row >= radius:
                beside = beside + now_ref[row - radius]
            if row + radius < rows:
                beside = beside + now_ref[row + radius]
            left = jnp.where(lane >= radius, pltpu.roll(centre, radius, 1), 0.0)
            right = jnp.where(lane < width - radius, pltpu.roll(centre, width - radius, 1), 0.0)
            bending = bending + STENCIL[radius] * (beside + (left + right))
        out_ref[row] = 2.0 * centre - prev_ref[row] + courant_ref[row] * (bending + own[row])


def deep_kernel(base_ref, above_ref, below_ref, courant_ref, out_ref):
    rows, depth, width = base_ref.shape
    at = lax.axis_index("depth")
    inside_above = (at != 0).astype(jnp.float32)
    inside_below = (at != lax.axis_size("depth") - 1).astype(jnp.float32)
    gap = jnp.zeros((depth - 2 * WIDTH, width), jnp.float32)
    for row in range(rows):
        above = above_ref[row] * inside_above
        below = below_ref[row] * inside_below
        upper, lower = [], []
        for layer in range(WIDTH):
            upper.append(
                sum(
                    STENCIL[radius] * above[WIDTH + layer - radius : WIDTH + layer - radius + 1]
                    for radius in range(layer + 1, WIDTH + 1)
                )
            )
            lower.append(
                sum(
                    STENCIL[radius] * below[layer + radius - WIDTH : layer + radius - WIDTH + 1]
                    for radius in range(WIDTH - layer, WIDTH + 1)
                )
            )
        bending = jnp.concatenate(upper + [gap] + lower, axis=0)
        out_ref[row] = base_ref[row] + courant_ref[row] * bending


def deep_layers(edges):
    count = lax.axis_size("depth")
    if count == 2:
        other = lax.ppermute(edges[0], "depth", [(0, 1), (1, 0)])
        return other, other
    return (
        lax.ppermute(edges[0], "depth", [(i, i + 1) for i in range(count - 1)]),
        lax.ppermute(edges[1], "depth", [(i + 1, i) for i in range(count - 1)]),
    )


def on_device(half_span, image, offset_of, background, wave_now, wave_prev, courant):
    groups = lax.axis_size("off")
    own_slab, prev = background[0], wave_prev[0]

    def sent(cells, step):
        return lax.ppermute(cells, "off", [(i, (i + step) % groups) for i in range(groups)])

    order = sorted(range(1, groups), key=lambda step: min(step, groups - step))
    slabs = {step: sent(own_slab, step) for step in order[:2]}
    held = pltpu.with_memory_space_constraint(image, pltpu.VMEM)
    now, cells, own_slab = moved(
        image,
        (wave_now[0], pltpu.VMEM),
        (offset_of, pltpu.SMEM),
        (own_slab, pltpu.VMEM),
    )
    slabs.update({step: sent(own_slab, step) for step in order[2:]})
    rows, depth, width = now.shape

    returned = {}
    part = now
    for step in order:
        edges = 0 if step != order[0] else 1 if lax.axis_size("depth") == 2 else 2
        part, *rest = source_of(
            held, cells, slabs[step], now, part, step, groups, half_span, edges
        )
        if edges:
            above, below = deep_layers(rest)
        back = [(i, (i - step) % groups) for i in range(groups)]
        returned[step] = lax.ppermute(part.astype(jnp.float16), "off", back).astype(jnp.float32)
    returned = [returned[step] for step in range(1, groups)]

    base = pl.pallas_call(
        functools.partial(step_kernel, half_span),
        out_shape=pltpu.VMEM(now.shape, jnp.float32),
        in_specs=[SMEM] + [VMEM] * 5,
        out_specs=VMEM,
        scratch_shapes=[pltpu.VMEM((rows, depth + 4 * WIDTH, width), jnp.float32)],
        compiler_params=pltpu.CompilerParams(vmem_limit_bytes=32 * MIB),
        cost_estimate=COST,
    )(cells, held, own_slab, now, prev, courant)
    base = pl.pallas_call(
        deep_kernel,
        out_shape=pltpu.VMEM(now.shape, jnp.float32),
        in_specs=[VMEM] * 4,
        out_specs=VMEM,
        compiler_params=pltpu.CompilerParams(vmem_limit_bytes=32 * MIB),
        cost_estimate=COST,
    )(base, above, below, courant)

    at = rows if groups > 2 else rows + WIDTH
    after, before = returned[0][rows : rows + WIDTH], returned[-1][at : at + WIDTH]
    beside = jnp.concatenate([before, jnp.zeros_like(now), after], axis=0)
    sums = functools.reduce(jnp.add, [part[:rows] for part in reversed(returned)])
    for radius in range(1, WIDTH + 1):
        sums = sums + STENCIL[radius] * (
            beside[WIDTH - radius : WIDTH - radius + rows]
            + beside[WIDTH + radius : WIDTH + radius + rows]
        )
    return (base + courant * (sums * (1.0 / SCALE)))[None]


def solution(mesh):
    def whole(image, offset_of, background, wave_now, wave_prev, courant):
        half_span = offset_of.shape[0] // 2
        assert half_span < LANES and background.shape[-1] % LANES == 0
        return jax.shard_map(
            functools.partial(on_device, half_span),
            mesh=mesh,
            in_specs=(
                P("off", None, "depth", None),
                P("off"),
                P(("parts", "shot"), "off", "depth", None),
                P(("parts", "shot"), "off", "depth", None),
                P(("parts", "shot"), "off", "depth", None),
                P("off", "depth", None),
            ),
            out_specs=P(("parts", "shot"), "off", "depth", None),
            check_vma=False,
        )(image, offset_of, background, wave_now, wave_prev, courant)

    return whole
```
